32 devices in a mesh: tm: 2 (over core), rows: 16 (over z, y, x).
Axes of the slice: x: 2, y: 2, z: 4, core: 2. Of those that a mesh axis runs over, the one named last changes fastest.
Arguments:
- feat: bfloat16 [4, 32, 240, 512], P('tm', 'rows'), may hold values from -24 to 24
- norm1_gain: float32 [512], replicated, may hold values from 0.5 to 1.5
- norm1_bias: float32 [512], replicated, may hold values from -3 to 3
- conv_weight: bfloat16 [3, 3, 3, 512, 512], replicated, may hold values from -0.0546875 to 0.0546875
- conv_bias: float32 [512], replicated, may hold values from -3 to 3
- norm2_gain: float32 [512], replicated, may hold values from 0.5 to 1.5
- norm2_bias: float32 [512], replicated, may hold values from -3 to 3
- w_query: bfloat16 [512, 512], replicated, may hold values from -0.44194174 to 0.44194174
- w_key: bfloat16 [512, 512], replicated, may hold values from -1.5467961 to 1.5467961
- w_value: bfloat16 [512, 512], replicated, may hold values from -0.25 to 0.25
- w_out: bfloat16 [512, 512], replicated, may hold values from -0.25 to 0.25
- out_bias: float32 [512], replicated, may hold values from -3 to 3
Outputs:
- block_out: bfloat16 [4, 32, 240, 512], P('tm', 'rows')
The draws below stay inside these ranges and needn't reach their ends.
All inputs are finite; a program needn't handle non-finite values.
Results may differ from the reference program's by a relative error of at most 0.0062.
The reference program's roundings to bfloat16 on the way (of `act`, `resid`, `normed`, `query`, `weight` and `attn`) count: a program that leaves them out, or rounds other values in their place, can miss the bound.
Values may be sent and summed in bfloat16 or wider, within the bound.
A program may use at most 128 MiB of HBM per device.

```python
import math
import jax
import jax.numpy as jnp
from jax import lax

C = 512
GROUPS = 32
ROWS_DEV = 2
W = 240
RADIUS = 4
FR = 4
H = 32
N_ROWS = 16


def draw_feat(key, part):
    first = jax.random.fold_in(key, 31)
    second = jax.random.fold_in(key, 32)
    fourth = jax.random.fold_in(key, 34)
    fifth = jax.random.fold_in(key, 35)
    rows_float = jnp.arange(H, dtype=jnp.float32) / (H - 1)
    ramp = 1.0 + 2.0 * rows_float
    offset = jnp.clip(0.5 * jax.random.normal(second, (C,), jnp.float32), -2.0, 2.0)
    stripe_shift = jnp.repeat(jax.random.uniform(fourth, (H // ROWS_DEV,), jnp.float32, -5.0, 5.0), ROWS_DEV)
    frame_shift = jax.random.uniform(fifth, (FR,), jnp.float32, -2.0, 2.0)
    shifts = stripe_shift[None, :, None, None] + frame_shift[:, None, None, None]
    base = jnp.clip(jax.random.normal(first, (FR, H, W, C), jnp.float32), -5.0, 5.0)
    rising = 0.5 + 2.0 * rows_float
    values = base * ramp[None, :, None, None] + offset + rising[None, :, None, None] + shifts
    values = jnp.clip(values, -24.0, 24.0)
    return values.astype(jnp.bfloat16)


def query_key(key):
    base = jnp.clip(jax.random.normal(jax.random.fold_in(key, 11), (C, C), jnp.float32), -5.0, 5.0)
    noise = jnp.clip(jax.random.normal(jax.random.fold_in(key, 12), (C, C), jnp.float32), -5.0, 5.0)
    base = 2.0 * base / math.sqrt(C)
    noise = noise / math.sqrt(C)
    return (base, noise)


def draw_w_query(key, part):
    return query_key(key)[0].astype(jnp.bfloat16)


def draw_w_key(key, part):
    return query_key(key)[1].astype(jnp.bfloat16)


def gaussian(own_key, dims, deviation, most, kind=jnp.bfloat16):
    result = jax.random.normal(own_key, dims, jnp.float32) * deviation
    return jnp.minimum(jnp.maximum(result, -most), most).astype(kind)


def setup_inputs(seed: int = 0) -> dict:
    splits = jax.random.split(jax.random.key(seed), 13)
    return {
        "feat": draw_feat(jax.random.fold_in(splits[12], 71), 0),
        "norm1_gain": jnp.clip(jax.random.uniform(splits[1], (C,), jnp.float32, 0.5, 1.5), 0.5, 1.5),
        "norm1_bias": gaussian(splits[2], (C,), 0.5, 3.0, jnp.float32),
        "conv_weight": gaussian(splits[3], (3, 3, 3, C, C), (27 * C) ** -0.5, 0.0546875),
        "conv_bias": gaussian(splits[4], (C,), 0.5, 3.0, jnp.float32),
        "norm2_gain": jnp.clip(jax.random.uniform(splits[5], (C,), jnp.float32, 0.5, 1.5), 0.5, 1.5),
        "norm2_bias": gaussian(splits[6], (C,), 0.5, 3.0, jnp.float32),
        "w_query": draw_w_query(jax.random.fold_in(splits[12], 71), 0),
        "w_key": draw_w_key(jax.random.fold_in(splits[12], 71), 0),
        "w_value": gaussian(splits[9], (C, C), C ** -0.5, 0.25),
        "w_out": gaussian(splits[10], (C, C), C ** -0.5, 0.25),
        "out_bias": gaussian(splits[11], (C,), 0.5, 3.0, jnp.float32),
    }


EPS = 1e-06

def group_norm(values, gain, shift):
    chans = values.shape[-1]
    grouped = values.reshape(values.shape[:-1] + (GROUPS, chans // GROUPS))
    count = values.shape[0] * values.shape[1] * values.shape[2] * (chans // GROUPS)
    mean = lax.optimization_barrier(jnp.sum(grouped, axis=(0, 1, 2, 4))) / count
    centered = grouped - mean[:, None]
    spread = lax.optimization_barrier(jnp.sum(centered * centered, axis=(0, 1, 2, 4))) / count
    normed = centered * lax.rsqrt(spread + EPS)[:, None]
    return normed.reshape(values.shape) * gain + shift

def conv_taps(padded, weight, frames, height, width):
    chans = padded.shape[-1]
    total = jnp.zeros((frames * height * width, weight.shape[-1]), jnp.float32)
    for step_t in range(3):
        for step_h in range(3):
            slab = padded[step_t:step_t + frames, step_h:step_h + height]
            stacked = jnp.concatenate([slab[:, :, step_w:step_w + width] for step_w in range(3)], axis=-1)
            total = total + jnp.dot(stacked.reshape(-1, 3 * chans), weight[step_t, step_h].reshape(3 * chans, -1), preferred_element_type=jnp.float32)
    return total.reshape(frames, height, width, -1)

def attend(query, keys, values, valid):
    scale = 1.0 / math.sqrt(query.shape[-1])
    scores = jnp.einsum('fqc,fkc->fqk', query, keys, preferred_element_type=jnp.float32) * scale
    scores = jnp.where(valid[None, None, :], scores, jnp.float32(-1e+30))
    top = lax.optimization_barrier(jnp.max(scores, axis=-1, keepdims=True))
    expo = jnp.exp(scores - top)
    total = lax.optimization_barrier(jnp.sum(expo, axis=-1, keepdims=True))
    mixed = jnp.einsum('fqk,fkc->fqc', expo.astype(jnp.bfloat16), values, preferred_element_type=jnp.float32)
    return (mixed / total).astype(jnp.bfloat16)

def reference(feat, norm1_gain, norm1_bias, conv_weight, conv_bias, norm2_gain, norm2_bias, w_query, w_key, w_value, w_out, out_bias):
    frames, height, width, chans = feat.shape
    act = jax.nn.silu(group_norm(feat.astype(jnp.float32), norm1_gain, norm1_bias)).astype(jnp.bfloat16)
    timed = jnp.concatenate([act[:1], act[:1], act], axis=0)
    padded = jnp.pad(timed, ((0, 0), (1, 1), (1, 1), (0, 0)))
    conv = conv_taps(padded, conv_weight, frames, height, width) + conv_bias
    resid = (feat.astype(jnp.float32) + conv).astype(jnp.bfloat16)
    normed = group_norm(resid.astype(jnp.float32), norm2_gain, norm2_bias).astype(jnp.bfloat16)
    flat = normed.reshape(-1, chans)
    shape4 = (frames, height, width, chans)
    query = jnp.dot(flat, w_query, preferred_element_type=jnp.float32).astype(jnp.bfloat16).reshape(shape4)
    keys = jnp.dot(flat, w_key, preferred_element_type=jnp.float32).astype(jnp.bfloat16).reshape(shape4)
    values = jnp.dot(flat, w_value, preferred_element_type=jnp.float32).astype(jnp.bfloat16).reshape(shape4)
    reach = RADIUS * ROWS_DEV
    span = 2 * reach + ROWS_DEV
    keys_pad = jnp.pad(keys, ((0, 0), (reach, reach), (0, 0), (0, 0)))
    values_pad = jnp.pad(values, ((0, 0), (reach, reach), (0, 0), (0, 0)))
    offsets = jnp.arange(span, dtype=jnp.int32)

    def stripe(index):
        start = (index * ROWS_DEV).astype(jnp.int32)
        qblock = lax.dynamic_slice_in_dim(query, start, ROWS_DEV, 1).reshape(frames, -1, chans)
        kblock = lax.dynamic_slice_in_dim(keys_pad, start, span, 1).reshape(frames, -1, chans)
        vblock = lax.dynamic_slice_in_dim(values_pad, start, span, 1).reshape(frames, -1, chans)
        place = start - reach + offsets
        valid = jnp.repeat((place >= 0) & (place < height), width)
        return attend(qblock, kblock, vblock, valid)
    blocks = lax.map(stripe, jnp.arange(N_ROWS, dtype=jnp.int32))
    attn = blocks.reshape(N_ROWS, frames, ROWS_DEV, width, chans).transpose(1, 0, 2, 3, 4).reshape(-1, chans)
    mixed = jnp.dot(attn, w_out, preferred_element_type=jnp.float32).reshape(shape4)
    return (resid.astype(jnp.float32) + out_bias + mixed).astype(jnp.bfloat16)
```

```python
import functools
import math

import jax
import jax.numpy as jnp
from jax import lax
from jax.experimental import pallas as pl
from jax.experimental.pallas import tpu as pltpu
from jax.sharding import PartitionSpec as P

GROUPS = 32
EPS = 1e-06
BAND = 4
MESH = pl.DeviceIdType.MESH
VMEM_LIMIT = 56 * 1024 * 1024


def greet_all(count, stripes, me):
    barrier = pltpu.get_barrier_semaphore()

    def greet(step, carry):
        peer = (me + step) % count
        pl.semaphore_signal(
            barrier, inc=1, device_id=(peer // stripes, peer % stripes), device_id_type=MESH
        )
        return carry

    lax.fori_loop(1, count, greet, 0)
    pl.semaphore_wait(barrier, count - 1)


def send_stats(count, stripes, me, stat_ref, all_ref, send_sem, recv_sem):
    all_ref[me] = stat_ref[0]

    def send(step, carry):
        peer = (me + step) % count
        pltpu.make_async_remote_copy(
            src_ref=stat_ref.at[0],
            dst_ref=all_ref.at[me],
            send_sem=send_sem,
            recv_sem=recv_sem,
            device_id=(peer // stripes, peer % stripes),
            device_id_type=MESH,
        ).start()
        return carry

    lax.fori_loop(1, count, send, 0)


def wait_stats(count, all_ref, send_sem, recv_sem):
    others = all_ref.at[pl.ds(0, count - 1)]
    pltpu.make_async_copy(others, others, recv_sem).wait()
    pltpu.make_async_copy(others, others, send_sem).wait()


def stats_kernel(sections, stripes, stat_ref, all_ref, send_sem, recv_sem):
    count = sections * stripes
    me = lax.axis_index("tm") * stripes + lax.axis_index("rows")
    greet_all(count, stripes, me)
    send_stats(count, stripes, me, stat_ref, all_ref, send_sem, recv_sem)
    wait_stats(count, all_ref, send_sem, recv_sem)


def halo_kernel(
    sections,
    stripes,
    stat_ref,
    feat_ref,
    all_ref,
    ext_ref,
    send_sem,
    recv_sem,
    local_sem,
    out_sem,
    in_sem,
):
    count = sections * stripes
    tm = lax.axis_index("tm")
    row = lax.axis_index("rows")
    me = tm * stripes + row
    frames, high = feat_ref.shape[:2]
    own = pltpu.make_async_copy(
        feat_ref, ext_ref.at[pl.ds(frames, frames), pl.ds(1, high)], local_sem
    )
    own.start()
    greet_all(count, stripes, me)
    send_stats(count, stripes, me, stat_ref, all_ref, send_sem, recv_sem)

    def push(src, dst, slot, to_tm, to_row):
        return pltpu.make_async_remote_copy(
            src_ref=src,
            dst_ref=dst,
            send_sem=out_sem.at[slot],
            recv_sem=in_sem.at[slot],
            device_id=(to_tm, to_row),
            device_id_type=MESH,
        )

    now = pl.ds(frames, frames)
    past = pl.ds(0, frames)
    down = push(feat_ref.at[:, high - 1], ext_ref.at[now, 0], 0, tm, row + 1)
    up = push(feat_ref.at[:, 0], ext_ref.at[now, high + 1], 1, tm, row - 1)
    later = push(feat_ref, ext_ref.at[past, pl.ds(1, high)], 2, tm + 1, row)
    later_top = push(ext_ref.at[now, 0], ext_ref.at[past, 0], 3, tm + 1, row)
    later_low = push(ext_ref.at[now, high + 1], ext_ref.at[past, high + 1], 4, tm + 1, row)
    has_next = tm < sections - 1
    has_past = tm > 0
    has_above = row > 0
    has_below = row < stripes - 1

    pl.when(has_below)(lambda: down.start())
    pl.when(has_above)(lambda: up.start())
    pl.when(has_next)(lambda: later.start())

    @pl.when(has_above)
    def _():
        down.wait_recv()
        pl.when(has_next)(lambda: later_top.start())

    @pl.when(has_below)
    def _():
        up.wait_recv()
        pl.when(has_next)(lambda: later_low.start())

    @pl.when(has_past)
    def _():
        later.wait_recv()
        pl.when(has_above)(lambda: later_top.wait_recv())
        pl.when(has_below)(lambda: later_low.wait_recv())

    pl.when(has_below)(lambda: down.wait_send())
    pl.when(has_above)(lambda: up.wait_send())

    @pl.when(has_next)
    def _():
        later.wait_send()
        pl.when(has_above)(lambda: later_top.wait_send())
        pl.when(has_below)(lambda: later_low.wait_send())

    own.wait()
    wait_stats(count, all_ref, send_sem, recv_sem)


def attend_kernel(
    stripes,
    normed_ref,
    wq_ref,
    wk_ref,
    wv_ref,
    out_ref,
    window,
    query,
    key,
    value,
    top,
    total,
    mixed,
    reply,
    in_sem,
    out_sem,
    back_in,
    back_out,
):
    bands = stripes // BAND
    tm = lax.axis_index("tm")
    row = lax.axis_index("rows")
    band = row // BAND
    k = row % BAND
    first = band * BAND
    cells, chans = normed_ref.shape[1:]
    scale = 1.0 / math.sqrt(chans)
    has_above = band > 0
    has_below = band < bands - 1
    half = k // 2

    barrier = pltpu.get_barrier_semaphore()

    def greet(to_tm, to_row):
        pl.semaphore_signal(barrier, inc=1, device_id=(to_tm, to_row), device_id_type=MESH)

    greet(1 - tm, row)
    pl.when(has_above)(lambda: greet(tm, row - BAND))
    pl.when(has_below)(lambda: greet(tm, row + BAND))
    for j in range(2):
        pl.when(2 * tm + j != k)(lambda j=j: greet(half, first + 2 * tm + j))
    peers = 1 + has_above.astype(jnp.int32) + has_below.astype(jnp.int32)
    for j in range(2):
        peers = peers + (2 * tm + j != k).astype(jnp.int32)
    pl.semaphore_wait(barrier, peers)

    def push(src, dst, sent, got, to_tm, to_row):
        return pltpu.make_async_remote_copy(
            src_ref=src,
            dst_ref=dst,
            send_sem=sent,
            recv_sem=got,
            device_id=(to_tm, to_row),
            device_id_type=MESH,
        )

    def scatter(j):
        return push(
            normed_ref.at[j],
            window.at[BAND + k],
            out_sem.at[j],
            in_sem.at[BAND + k],
            half,
            first + 2 * tm + j,
        )

    for j in range(2):
        pl.when(2 * tm + j != k)(lambda j=j: scatter(j).start())

        @pl.when(2 * tm + j == k)
        def _(j=j):
            pltpu.make_async_copy(
                normed_ref.at[j], window.at[BAND + k], in_sem.at[BAND + k]
            ).start()

    def arrived(slot):
        pltpu.make_async_copy(window.at[slot], window.at[slot], in_sem.at[slot]).wait()

    def across(slot, number):
        return push(
            window.at[slot],
            window.at[slot],
            out_sem.at[number],
            in_sem.at[slot],
            1 - tm,
            row,
        )

    def downward(slot, number):
        return push(
            window.at[slot],
            window.at[slot - BAND],
            out_sem.at[number],
            in_sem.at[slot - BAND],
            tm,
            row + BAND,
        )

    def upward(slot, number):
        return push(
            window.at[slot],
            window.at[slot + BAND],
            out_sem.at[number],
            in_sem.at[slot + BAND],
            tm,
            row - BAND,
        )

    def update(q, slot):
        scores = (
            lax.dot_general(
                query[q], key[...], (((1,), (1,)), ((), ())), preferred_element_type=jnp.float32
            )
            * scale
        )
        old = top[q]
        new = jnp.maximum(old, jnp.max(scores, axis=-1, keepdims=True))
        expo = jnp.exp(scores - new[:, :1])
        shrink = jnp.exp(old - new)
        total[q] = total[q] * shrink + jnp.sum(expo, axis=-1, keepdims=True)
        top[q] = new
        mixed[q] = mixed[q] * shrink[:, :1] + jnp.dot(
            expo.astype(jnp.bfloat16), value[...], preferred_element_type=jnp.float32
        )

    def queries(t, carry):
        slot = BAND + 2 * tm + t
        arrived(slot)
        pl.when(has_below)(lambda: downward(slot, 2 + t).start())
        pl.when(has_above)(lambda: upward(slot, 4 + t).start())
        across(slot, 6 + t).start()
        query[t] = jnp.dot(window[slot], wq_ref[...], preferred_element_type=jnp.float32).astype(
            jnp.bfloat16
        )
        top[t] = jnp.full_like(top[t], -1e30)
        total[t] = jnp.zeros_like(total[t])
        mixed[t] = jnp.zeros_like(mixed[t])
        return carry

    lax.fori_loop(0, 2, queries, 0)

    def slots(t, carry):
        stage = t // 2
        i = t % 2
        slot = i + jnp.where(
            stage == 0,
            BAND + 2 * tm,
            jnp.where(
                stage == 1,
                BAND + 2 * (1 - tm),
                jnp.where(stage == 2, 2 * tm, jnp.where(stage == 3, 2 * BAND + 2 * tm, 2 + 6 * tm)),
            ),
        )
        inside = ((slot >= BAND) | has_above) & ((slot < 2 * BAND) | has_below)

        @pl.when(inside)
        def _():
            pl.when(stage > 0)(lambda: arrived(slot))
            pl.when((stage == 2) & (tm == 1))(lambda: across(slot, 8 + i).start())
            pl.when((stage == 3) & (tm == 0))(lambda: across(slot, 8 + i).start())
            key[...] = jnp.dot(
                window[slot], wk_ref[...], preferred_element_type=jnp.float32
            ).astype(jnp.bfloat16)
            value[...] = jnp.dot(
                window[slot], wv_ref[...], preferred_element_type=jnp.float32
            ).astype(jnp.bfloat16)

            def one(q, inner):
                start = 2 * tm + q
                pl.when((slot >= start) & (slot <= start + 2 * BAND))(lambda: update(q, slot))
                return inner

            lax.fori_loop(0, 2, one, 0)

        return carry

    lax.fori_loop(0, 10, slots, 0)

    def answer(q):
        return push(
            reply.at[q], out_ref.at[k % 2], back_out.at[q], back_in.at[k % 2], half, first + 2 * tm + q
        )

    for q in range(2):
        reply[q] = (mixed[q] / total[q][:, :1]).astype(jnp.bfloat16)
        pl.when(2 * tm + q != k)(lambda q=q: answer(q).start())

        @pl.when(2 * tm + q == k)
        def _(q=q):
            pltpu.make_async_copy(reply.at[q], out_ref.at[k % 2], back_in.at[k % 2]).start()

    for j in range(2):
        pltpu.make_async_copy(out_ref.at[j], out_ref.at[j], back_in.at[j]).wait()

        @pl.when(2 * tm + j != k)
        def _(j=j):
            scatter(j).wait_send()
            answer(j).wait_send()

        across(BAND + 2 * tm + j, 6 + j).wait_send()
        pl.when(has_below)(lambda j=j: downward(BAND + 2 * tm + j, 2 + j).wait_send())
        pl.when(has_above)(lambda j=j: upward(BAND + 2 * tm + j, 4 + j).wait_send())
        pl.when((tm == 1) & has_above)(lambda j=j: across(2 + j, 8 + j).wait_send())
        pl.when((tm == 0) & has_below)(lambda j=j: across(2 * BAND + j, 8 + j).wait_send())


def local_stats(values):
    chans = values.shape[-1]
    grouped = values.reshape(-1, GROUPS, chans // GROUPS)
    size = grouped.shape[0] * grouped.shape[2]
    mean = jnp.sum(grouped, axis=(0, 2)) / size
    centered = grouped - mean[:, None]
    spread = jnp.sum(centered * centered, axis=(0, 2))
    packed = jnp.concatenate([mean, spread, jnp.zeros((128 - 2 * GROUPS,), jnp.float32)])
    return packed.reshape(1, 1, 128), size


def norm_terms(stats, size, gain, shift):
    means = stats[:, 0, :GROUPS]
    spreads = stats[:, 0, GROUPS : 2 * GROUPS]
    mean = jnp.mean(means, axis=0)
    gap = means - mean
    spread = jnp.sum(spreads + size * gap * gap, axis=0) / (size * stats.shape[0])
    each = gain.shape[0] // GROUPS
    return jnp.repeat(mean, each), jnp.repeat(lax.rsqrt(spread + EPS), each) * gain, shift


def normalize(values, terms):
    mean, gain, shift = terms
    return (values - mean) * gain + shift


def conv_taps(padded, weight, frames, height, width):
    chans = padded.shape[-1]
    total = jnp.zeros((frames * height * width, weight.shape[-1]), jnp.float32)
    for step_t in range(3):
        for step_h in range(3):
            slab = padded[step_t : step_t + frames, step_h : step_h + height]
            stacked = jnp.concatenate(
                [slab[:, :, step_w : step_w + width] for step_w in range(3)], axis=-1
            )
            total = total + jnp.dot(
                stacked.reshape(-1, 3 * chans),
                weight[step_t, step_h].reshape(3 * chans, -1),
                preferred_element_type=jnp.float32,
            )
    return total.reshape(frames, height, width, -1)


def shards(
    feat,
    norm1_gain,
    norm1_bias,
    conv_weight,
    conv_bias,
    norm2_gain,
    norm2_bias,
    w_query,
    w_key,
    w_value,
    w_out,
    out_bias,
):
    frames, high, width, chans = feat.shape
    sections = lax.axis_size("tm")
    stripes = lax.axis_size("rows")
    count = sections * stripes
    row = lax.axis_index("rows")
    vmem = pl.BlockSpec(memory_space=pltpu.VMEM)
    anywhere = pl.BlockSpec(memory_space=pl.ANY)
    all_stats = jax.ShapeDtypeStruct((count, 1, 128), jnp.float32)
    dma = pltpu.SemaphoreType.DMA

    stat1, size = local_stats(feat.astype(jnp.float32))
    stats1, ext = pl.pallas_call(
        functools.partial(halo_kernel, sections, stripes),
        out_shape=(
            all_stats,
            jax.ShapeDtypeStruct((2 * frames, high + 2, width, chans), jnp.bfloat16),
        ),
        in_specs=[vmem, anywhere],
        out_specs=(vmem, anywhere),
        scratch_shapes=[dma, dma, dma, dma((5,)), dma((5,))],
        compiler_params=pltpu.CompilerParams(collective_id=0, has_side_effects=True),
        name="halo",
    )(stat1, feat)
    act = jax.nn.silu(
        normalize(ext.astype(jnp.float32), norm_terms(stats1, size, norm1_gain, norm1_bias))
    ).astype(jnp.bfloat16)
    opening = jnp.broadcast_to(act[frames : frames + 1], act[:frames].shape)
    past = jnp.where(lax.axis_index("tm") == 0, opening, act[:frames])
    timed = jnp.concatenate([past, act[frames:]], axis=0)
    place = row * high - 1 + jnp.arange(high + 2, dtype=jnp.int32)
    within = (place >= 0) & (place < stripes * high)
    timed = jnp.where(within[None, :, None, None], timed, jnp.bfloat16(0))
    padded = jnp.pad(timed, ((0, 0), (0, 0), (1, 1), (0, 0)))
    conv = conv_taps(padded, conv_weight, frames, high, width) + conv_bias
    resid = (feat.astype(jnp.float32) + conv).astype(jnp.bfloat16)

    stat2, size = local_stats(resid.astype(jnp.float32))
    stats2 = pl.pallas_call(
        functools.partial(stats_kernel, sections, stripes),
        out_shape=all_stats,
        in_specs=[vmem],
        out_specs=vmem,
        scratch_shapes=[dma, dma],
        compiler_params=pltpu.CompilerParams(collective_id=1, has_side_effects=True),
        name="stats",
    )(stat2)
    normed = normalize(
        resid.astype(jnp.float32), norm_terms(stats2, size, norm2_gain, norm2_bias)
    ).astype(jnp.bfloat16)
    cells = high * width
    attn = pl.pallas_call(
        functools.partial(attend_kernel, stripes),
        out_shape=jax.ShapeDtypeStruct((frames, cells, chans), jnp.bfloat16),
        in_specs=[vmem] * 4,
        out_specs=vmem,
        scratch_shapes=[
            pltpu.VMEM((3 * BAND, cells, chans), jnp.bfloat16),
            pltpu.VMEM((2, cells, chans), jnp.bfloat16),
            pltpu.VMEM((cells, chans), jnp.bfloat16),
            pltpu.VMEM((cells, chans), jnp.bfloat16),
            pltpu.VMEM((2, cells, 128), jnp.float32),
            pltpu.VMEM((2, cells, 128), jnp.float32),
            pltpu.VMEM((2, cells, chans), jnp.float32),
            pltpu.VMEM((2, cells, chans), jnp.bfloat16),
            dma((3 * BAND,)),
            dma((10,)),
            dma((2,)),
            dma((2,)),
        ],
        compiler_params=pltpu.CompilerParams(
            collective_id=2, has_side_effects=True, vmem_limit_bytes=VMEM_LIMIT
        ),
        name="attend",
    )(normed.reshape(frames, cells, chans), w_query, w_key, w_value)
    output = jnp.dot(
        attn.reshape(-1, chans), w_out, preferred_element_type=jnp.float32
    ).reshape(frames, high, width, chans)
    return (resid.astype(jnp.float32) + out_bias + output).astype(jnp.bfloat16)


def solution(mesh):
    return jax.shard_map(
        shards,
        mesh=mesh,
        in_specs=(
            P("tm", "rows", None, None),
            P(),
            P(),
            P(),
            P(),
            P(),
            P(),
            P(),
            P(),
            P(),
            P(),
            P(),
        ),
        out_specs=P("tm", "rows", None, None),
        check_vma=False,
    )
```

```python
import functools
import math

import jax
import jax.numpy as jnp
from jax import lax
from jax.experimental import pallas as pl
from jax.experimental.pallas import tpu as pltpu
from jax.sharding import PartitionSpec as P

GROUPS = 32
EPS = 1e-06
BAND = 4
MESH = pl.DeviceIdType.MESH
VMEM_LIMIT = 56 * 1024 * 1024


def greet_all(count, stripes, me):
    barrier = pltpu.get_barrier_semaphore()

    def greet(step, carry):
        peer = (me + step) % count
        pl.semaphore_signal(
            barrier, inc=1, device_id=(peer // stripes, peer % stripes), device_id_type=MESH
        )
        return carry

    lax.fori_loop(1, count, greet, 0)
    pl.semaphore_wait(barrier, count - 1)


def group_total(values):
    chans = values.shape[-1]
    each = chans // GROUPS
    lane = lax.broadcasted_iota(jnp.int32, values.shape, 1)
    step = 1
    while step < each:
        ahead = pltpu.roll(values, chans - step, 1)
        behind = pltpu.roll(values, step, 1)
        values = values + jnp.where((lane // step) % 2 == 0, ahead, behind)
        step *= 2
    return values


def rows_of_8(line):
    return jnp.broadcast_to(line, (8, line.shape[-1]))


def is_mean_lane(shape):
    each = shape[-1] // GROUPS
    return lax.broadcasted_iota(jnp.int32, shape, 1) % each < each // 2


def share_stats(count, stripes, me, blocks, all_ref, send_sem, recv_sem):
    first = blocks[0]()
    chans = first.shape[-1]
    size = len(blocks) * first.shape[0] * (chans // GROUPS)
    total = jnp.sum(first, axis=0, keepdims=True)
    for block in blocks[1:]:
        total = total + jnp.sum(block(), axis=0, keepdims=True)
    mean = group_total(rows_of_8(total)) / size
    spread = jnp.zeros((1, chans), jnp.float32)
    for block in blocks:
        gap = block() - mean[:1]
        spread = spread + jnp.sum(gap * gap, axis=0, keepdims=True)
    spread = group_total(rows_of_8(spread))
    all_ref[me] = jnp.where(is_mean_lane(mean.shape), mean, spread)[:1]

    def send(step, carry):
        peer = (me + step) % count
        pltpu.make_async_remote_copy(
            src_ref=all_ref.at[me],
            dst_ref=all_ref.at[me],
            send_sem=send_sem,
            recv_sem=recv_sem,
            device_id=(peer // stripes, peer % stripes),
            device_id_type=MESH,
        ).start()
        return carry

    lax.fori_loop(1, count, send, 0)
    return size


def norm_terms(count, size, all_ref, send_sem, recv_sem, gain):
    others = all_ref.at[pl.ds(0, count - 1)]
    pltpu.make_async_copy(others, others, recv_sem).wait()
    pltpu.make_async_copy(others, others, send_sem).wait()
    stats = all_ref[...]
    chans = stats.shape[-1]
    half = chans // GROUPS // 2
    total = jnp.sum(stats, axis=0)
    gap = stats - total / count
    gaps = jnp.sum(gap * gap, axis=0)
    total = rows_of_8(total)
    gaps = rows_of_8(gaps)
    means = is_mean_lane(total.shape)
    mean = group_total(jnp.where(means, total, 0.0)) / (half * count)
    spread = group_total(jnp.where(means, gaps * size, total)) / half / (size * count)
    return mean[:1], (lax.rsqrt(spread + EPS) * gain)[:1]


def conv_kernel(
    sections,
    stripes,
    feat_ref,
    gain1_ref,
    bias1_ref,
    weight_ref,
    bias_ref,
    gain2_ref,
    bias2_ref,
    resid_ref,
    normed_ref,
    ext,
    act,
    weight,
    conv,
    all1,
    all2,
    stat_sem,
    weight_sem,
    out_sem,
    in_sem,
):
    count = sections * stripes
    tm = lax.axis_index("tm")
    row = lax.axis_index("rows")
    me = tm * stripes + row
    frames, high, width, chans = feat_ref.shape
    has_next = tm < sections - 1
    has_past = tm > 0
    has_above = row > 0
    has_below = row < stripes - 1

    loads = [
        pltpu.make_async_copy(weight_ref.at[a], weight.at[a], weight_sem.at[a]) for a in range(3)
    ]
    for load in loads:
        load.start()
    greet_all(count, stripes, me)

    def push(src, dst, slot, to_tm, to_row):
        return pltpu.make_async_remote_copy(
            src_ref=src,
            dst_ref=dst,
            send_sem=out_sem.at[slot],
            recv_sem=in_sem.at[slot],
            device_id=(to_tm, to_row),
            device_id_type=MESH,
        )

    now = pl.ds(frames, frames)
    past = pl.ds(0, frames)
    down = push(feat_ref.at[:, high - 1], ext.at[now, 0], 0, tm, row + 1)
    up = push(feat_ref.at[:, 0], ext.at[now, high + 1], 1, tm, row - 1)
    later = push(feat_ref, ext.at[past, pl.ds(1, high)], 2, tm + 1, row)
    later_top = push(ext.at[now, 0], ext.at[past, 0], 3, tm + 1, row)
    later_low = push(ext.at[now, high + 1], ext.at[past, high + 1], 4, tm + 1, row)

    pl.when(has_below)(lambda: down.start())
    pl.when(has_above)(lambda: up.start())
    pl.when(has_next)(lambda: later.start())

    blocks = [
        lambda f=f, o=o: feat_ref[f, o].astype(jnp.float32)
        for f in range(frames)
        for o in range(high)
    ]
    size = share_stats(count, stripes, me, blocks, all1, stat_sem.at[0], stat_sem.at[1])
    mean1, gain1 = norm_terms(count, size, all1, stat_sem.at[0], stat_sem.at[1], gain1_ref[...])
    bias1 = bias1_ref[...]
    column = lax.broadcasted_iota(jnp.int32, (width, chans), 0)

    def activate(source, targets):
        scaled = (source.astype(jnp.float32) - mean1) * gain1 + bias1
        half = 0.5 * scaled
        silu = half + half * jnp.tanh(half)
        before = jnp.where(column == 0, 0.0, pltpu.roll(silu, 1, 0)).astype(jnp.bfloat16)
        after = jnp.where(column == width - 1, 0.0, pltpu.roll(silu, width - 1, 0)).astype(
            jnp.bfloat16
        )
        here = silu.astype(jnp.bfloat16)
        for f, r in targets:
            act[f, r, :, :chans] = before
            act[f, r, :, chans : 2 * chans] = here
            act[f, r, :, 2 * chans :] = after

    def open_frames(r):
        for f in range(frames):
            act[f, r] = act[frames, r]

    for r in range(1, high + 1):
        for f in range(frames):
            activate(feat_ref[f, r - 1], [(frames + f, r)])
    pl.when(tm == 0)(lambda: [open_frames(r) for r in range(1, high + 1)] and None)

    @pl.when(has_past)
    def _():
        later.wait_recv()

        def earlier(index, carry):
            f = index // high
            r = 1 + index % high
            activate(ext[f, r], [(f, r)])
            return carry

        lax.fori_loop(0, frames * high, earlier, 0)

    cells = frames * width

    def taps(a, r, b):
        return jnp.dot(
            act[pl.ds(a, frames), r].reshape(cells, 3 * chans),
            weight[a, b],
            preferred_element_type=jnp.float32,
        ).reshape(frames, width, chans)

    conv[...] = jnp.broadcast_to(bias_ref[...].reshape(1, 1, 1, chans), conv.shape)

    def inner(a, carry):
        conv[:, 0] += taps(a, 1, 1) + taps(a, 2, 2)
        conv[:, 1] += taps(a, 1, 0) + taps(a, 2, 1)
        return carry

    for a in range(3):
        loads[a].wait()
    lax.fori_loop(0, 2, inner, 0)

    @pl.when(has_above)
    def _():
        down.wait_recv()
        pl.when(has_next)(lambda: later_top.start())

    @pl.when(has_below)
    def _():
        up.wait_recv()
        pl.when(has_next)(lambda: later_low.start())

    lax.fori_loop(2, 3, inner, 0)

    def halo(r, exists, relay):
        @pl.when(exists)
        def _():
            def each(f, carry):
                activate(ext[frames + f, r], [(frames + f, r)])
                return carry

            lax.fori_loop(0, frames, each, 0)
            pl.when(tm == 0)(lambda: open_frames(r))

            @pl.when(has_past)
            def _():
                relay.wait_recv()

                def each_past(f, carry):
                    activate(ext[f, r], [(f, r)])
                    return carry

                lax.fori_loop(0, frames, each_past, 0)

        @pl.when(jnp.logical_not(exists))
        def _():
            act[:, r] = jnp.zeros_like(act[:, r])

    halo(0, has_above, later_top)
    halo(high + 1, has_below, later_low)

    def outer(a, carry):
        conv[:, 0] += taps(a, 0, 0)
        conv[:, 1] += taps(a, high + 1, 2)
        return carry

    lax.fori_loop(0, 3, outer, 0)

    for f in range(frames):
        for o in range(high):
            resid_ref[f, o] = (feat_ref[f, o].astype(jnp.float32) + conv[f, o]).astype(jnp.bfloat16)
    blocks = [
        lambda f=f, o=o: resid_ref[f, o].astype(jnp.float32)
        for f in range(frames)
        for o in range(high)
    ]
    size = share_stats(count, stripes, me, blocks, all2, stat_sem.at[2], stat_sem.at[3])

    pl.when(has_below)(lambda: down.wait_send())
    pl.when(has_above)(lambda: up.wait_send())

    @pl.when(has_next)
    def _():
        later.wait_send()
        pl.when(has_above)(lambda: later_top.wait_send())
        pl.when(has_below)(lambda: later_low.wait_send())

    mean2, gain2 = norm_terms(count, size, all2, stat_sem.at[2], stat_sem.at[3], gain2_ref[...])
    for f in range(frames):
        for o in range(high):
            normed_ref[f, o] = (
                (resid_ref[f, o].astype(jnp.float32) - mean2) * gain2 + bias2_ref[...]
            ).astype(jnp.bfloat16)


def attend_kernel(
    stripes,
    normed_ref,
    wq_ref,
    wk_ref,
    wv_ref,
    out_ref,
    window,
    query,
    key,
    value,
    top,
    total,
    mixed,
    reply,
    in_sem,
    out_sem,
    back_in,
    back_out,
):
    bands = stripes // BAND
    tm = lax.axis_index("tm")
    row = lax.axis_index("rows")
    band = row // BAND
    k = row % BAND
    first = band * BAND
    cells, chans = normed_ref.shape[1:]
    scale = 1.0 / math.sqrt(chans)
    has_above = band > 0
    has_below = band < bands - 1
    half = k // 2

    barrier = pltpu.get_barrier_semaphore()

    def greet(to_tm, to_row):
        pl.semaphore_signal(barrier, inc=1, device_id=(to_tm, to_row), device_id_type=MESH)

    greet(1 - tm, row)
    pl.when(has_above)(lambda: greet(tm, row - BAND))
    pl.when(has_below)(lambda: greet(tm, row + BAND))
    for j in range(2):
        pl.when(2 * tm + j != k)(lambda j=j: greet(half, first + 2 * tm + j))
    peers = 1 + has_above.astype(jnp.int32) + has_below.astype(jnp.int32)
    for j in range(2):
        peers = peers + (2 * tm + j != k).astype(jnp.int32)
    pl.semaphore_wait(barrier, peers)

    def push(src, dst, sent, got, to_tm, to_row):
        return pltpu.make_async_remote_copy(
            src_ref=src,
            dst_ref=dst,
            send_sem=sent,
            recv_sem=got,
            device_id=(to_tm, to_row),
            device_id_type=MESH,
        )

    def scatter(j):
        return push(
            normed_ref.at[j],
            window.at[BAND + k],
            out_sem.at[j],
            in_sem.at[BAND + k],
            half,
            first + 2 * tm + j,
        )

    for j in range(2):
        pl.when(2 * tm + j != k)(lambda j=j: scatter(j).start())

        @pl.when(2 * tm + j == k)
        def _(j=j):
            pltpu.make_async_copy(
                normed_ref.at[j], window.at[BAND + k], in_sem.at[BAND + k]
            ).start()

    def arrived(slot):
        pltpu.make_async_copy(window.at[slot], window.at[slot], in_sem.at[slot]).wait()

    def across(slot, number):
        return push(
            window.at[slot],
            window.at[slot],
            out_sem.at[number],
            in_sem.at[slot],
            1 - tm,
            row,
        )

    def downward(slot, number):
        return push(
            window.at[slot],
            window.at[slot - BAND],
            out_sem.at[number],
            in_sem.at[slot - BAND],
            tm,
            row + BAND,
        )

    def upward(slot, number):
        return push(
            window.at[slot],
            window.at[slot + BAND],
            out_sem.at[number],
            in_sem.at[slot + BAND],
            tm,
            row - BAND,
        )

    def update(q, slot):
        scores = (
            lax.dot_general(
                query[q], key[...], (((1,), (1,)), ((), ())), preferred_element_type=jnp.float32
            )
            * scale
        )
        old = top[q]
        new = jnp.maximum(old, jnp.max(scores, axis=-1, keepdims=True))
        expo = jnp.exp(scores - new[:, :1])
        shrink = jnp.exp(old - new)
        total[q] = total[q] * shrink + jnp.sum(expo, axis=-1, keepdims=True)
        top[q] = new
        mixed[q] = mixed[q] * shrink[:, :1] + jnp.dot(
            expo.astype(jnp.bfloat16), value[...], preferred_element_type=jnp.float32
        )

    def queries(t, carry):
        slot = BAND + 2 * tm + t
        arrived(slot)
        pl.when(has_below)(lambda: downward(slot, 2 + t).start())
        pl.when(has_above)(lambda: upward(slot, 4 + t).start())
        across(slot, 6 + t).start()
        query[t] = jnp.dot(window[slot], wq_ref[...], preferred_element_type=jnp.float32).astype(
            jnp.bfloat16
        )
        top[t] = jnp.full_like(top[t], -1e30)
        total[t] = jnp.zeros_like(total[t])
        mixed[t] = jnp.zeros_like(mixed[t])
        return carry

    lax.fori_loop(0, 2, queries, 0)

    def slots(t, carry):
        stage = t // 2
        i = t % 2
        slot = i + jnp.where(
            stage == 0,
            BAND + 2 * tm,
            jnp.where(
                stage == 1,
                BAND + 2 * (1 - tm),
                jnp.where(stage == 2, 2 * tm, jnp.where(stage == 3, 2 * BAND + 2 * tm, 2 + 6 * tm)),
            ),
        )
        inside = ((slot >= BAND) | has_above) & ((slot < 2 * BAND) | has_below)

        @pl.when(inside)
        def _():
            pl.when(stage > 0)(lambda: arrived(slot))
            pl.when((stage == 2) & (tm == 1))(lambda: across(slot, 8 + i).start())
            pl.when((stage == 3) & (tm == 0))(lambda: across(slot, 8 + i).start())
            key[...] = jnp.dot(
                window[slot], wk_ref[...], preferred_element_type=jnp.float32
            ).astype(jnp.bfloat16)
            value[...] = jnp.dot(
                window[slot], wv_ref[...], preferred_element_type=jnp.float32
            ).astype(jnp.bfloat16)

            def one(q, inner):
                start = 2 * tm + q
                pl.when((slot >= start) & (slot <= start + 2 * BAND))(lambda: update(q, slot))
                return inner

            lax.fori_loop(0, 2, one, 0)

        return carry

    lax.fori_loop(0, 10, slots, 0)

    def answer(q):
        return push(
            reply.at[q], out_ref.at[k % 2], back_out.at[q], back_in.at[k % 2], half, first + 2 * tm + q
        )

    for q in range(2):
        reply[q] = (mixed[q] / total[q][:, :1]).astype(jnp.bfloat16)
        pl.when(2 * tm + q != k)(lambda q=q: answer(q).start())

        @pl.when(2 * tm + q == k)
        def _(q=q):
            pltpu.make_async_copy(reply.at[q], out_ref.at[k % 2], back_in.at[k % 2]).start()

    for j in range(2):
        pltpu.make_async_copy(out_ref.at[j], out_ref.at[j], back_in.at[j]).wait()

        @pl.when(2 * tm + j != k)
        def _(j=j):
            scatter(j).wait_send()
            answer(j).wait_send()

        across(BAND + 2 * tm + j, 6 + j).wait_send()
        pl.when(has_below)(lambda j=j: downward(BAND + 2 * tm + j, 2 + j).wait_send())
        pl.when(has_above)(lambda j=j: upward(BAND + 2 * tm + j, 4 + j).wait_send())
        pl.when((tm == 1) & has_above)(lambda j=j: across(2 + j, 8 + j).wait_send())
        pl.when((tm == 0) & has_below)(lambda j=j: across(2 * BAND + j, 8 + j).wait_send())


def shards(
    feat,
    norm1_gain,
    norm1_bias,
    conv_weight,
    conv_bias,
    norm2_gain,
    norm2_bias,
    w_query,
    w_key,
    w_value,
    w_out,
    out_bias,
):
    frames, high, width, chans = feat.shape
    sections = lax.axis_size("tm")
    stripes = lax.axis_size("rows")
    count = sections * stripes
    vmem = pl.BlockSpec(memory_space=pltpu.VMEM)
    anywhere = pl.BlockSpec(memory_space=pl.ANY)
    dma = pltpu.SemaphoreType.DMA
    image = jax.ShapeDtypeStruct(feat.shape, jnp.bfloat16)
    resid, normed = pl.pallas_call(
        functools.partial(conv_kernel, sections, stripes),
        out_shape=(image, image),
        in_specs=[vmem, vmem, vmem, anywhere, vmem, vmem, vmem],
        out_specs=(vmem, vmem),
        scratch_shapes=[
            pltpu.VMEM((2 * frames, high + 2, width, chans), jnp.bfloat16),
            pltpu.VMEM((2 * frames, high + 2, width, 3 * chans), jnp.bfloat16),
            pltpu.VMEM((3, 3, 3 * chans, chans), jnp.bfloat16),
            pltpu.VMEM((frames, high, width, chans), jnp.float32),
            pltpu.VMEM((count, 1, chans), jnp.float32),
            pltpu.VMEM((count, 1, chans), jnp.float32),
            dma((4,)),
            dma((3,)),
            dma((5,)),
            dma((5,)),
        ],
        compiler_params=pltpu.CompilerParams(
            collective_id=0, has_side_effects=True, vmem_limit_bytes=VMEM_LIMIT
        ),
        name="conv",
    )(
        feat,
        norm1_gain[None],
        norm1_bias[None],
        conv_weight.reshape(3, 3, 3 * chans, chans),
        conv_bias[None],
        norm2_gain[None],
        norm2_bias[None],
    )
    cells = high * width
    attn = pl.pallas_call(
        functools.partial(attend_kernel, stripes),
        out_shape=jax.ShapeDtypeStruct((frames, cells, chans), jnp.bfloat16),
        in_specs=[vmem] * 4,
        out_specs=vmem,
        scratch_shapes=[
            pltpu.VMEM((3 * BAND, cells, chans), jnp.bfloat16),
            pltpu.VMEM((2, cells, chans), jnp.bfloat16),
            pltpu.VMEM((cells, chans), jnp.bfloat16),
            pltpu.VMEM((cells, chans), jnp.bfloat16),
            pltpu.VMEM((2, cells, 128), jnp.float32),
            pltpu.VMEM((2, cells, 128), jnp.float32),
            pltpu.VMEM((2, cells, chans), jnp.float32),
            pltpu.VMEM((2, cells, chans), jnp.bfloat16),
            dma((3 * BAND,)),
            dma((10,)),
            dma((2,)),
            dma((2,)),
        ],
        compiler_params=pltpu.CompilerParams(
            collective_id=2, has_side_effects=True, vmem_limit_bytes=VMEM_LIMIT
        ),
        name="attend",
    )(normed.reshape(frames, cells, chans), w_query, w_key, w_value)
    output = jnp.dot(
        attn.reshape(-1, chans), w_out, preferred_element_type=jnp.float32
    ).reshape(frames, high, width, chans)
    return (resid.astype(jnp.float32) + out_bias + output).astype(jnp.bfloat16)


def solution(mesh):
    return jax.shard_map(
        shards,
        mesh=mesh,
        in_specs=(
            P("tm", "rows", None, None),
            P(),
            P(),
            P(),
            P(),
            P(),
            P(),
            P(),
            P(),
            P(),
            P(),
            P(),
        ),
        out_specs=P("tm", "rows", None, None),
        check_vma=False,
    )
```

```python
import functools
import math

import jax
import jax.numpy as jnp
from jax import lax
from jax.experimental import pallas as pl
from jax.experimental.pallas import tpu as pltpu
from jax.sharding import PartitionSpec as P

GROUPS = 32
EPS = 1e-06
BAND = 4
MESH = pl.DeviceIdType.MESH
VMEM_LIMIT = 56 * 1024 * 1024


def greet_all(count, stripes, me):
    barrier = pltpu.get_barrier_semaphore()

    def greet(step, carry):
        peer = (me + step) % count
        pl.semaphore_signal(
            barrier, inc=1, device_id=(peer // stripes, peer % stripes), device_id_type=MESH
        )
        return carry

    lax.fori_loop(1, count, greet, 0)
    pl.semaphore_wait(barrier, count - 1)


def group_total(values):
    chans = values.shape[-1]
    each = chans // GROUPS
    lane = lax.broadcasted_iota(jnp.int32, values.shape, 1)
    step = 1
    while step < each:
        ahead = pltpu.roll(values, chans - step, 1)
        behind = pltpu.roll(values, step, 1)
        values = values + jnp.where((lane // step) % 2 == 0, ahead, behind)
        step *= 2
    return values


def rows_of_8(line):
    return jnp.broadcast_to(line, (8, line.shape[-1]))


def is_mean_lane(shape):
    each = shape[-1] // GROUPS
    return lax.broadcasted_iota(jnp.int32, shape, 1) % each < each // 2


def share_stats(count, stripes, me, blocks, all_ref, send_sem, recv_sem):
    first = blocks[0]()
    chans = first.shape[-1]
    size = len(blocks) * first.shape[0] * (chans // GROUPS)
    total = jnp.sum(first, axis=0, keepdims=True)
    for block in blocks[1:]:
        total = total + jnp.sum(block(), axis=0, keepdims=True)
    mean = group_total(rows_of_8(total)) / size
    spread = jnp.zeros((1, chans), jnp.float32)
    for block in blocks:
        gap = block() - mean[:1]
        spread = spread + jnp.sum(gap * gap, axis=0, keepdims=True)
    spread = group_total(rows_of_8(spread))
    all_ref[me] = jnp.where(is_mean_lane(mean.shape), mean, spread)[:1]

    def send(step, carry):
        peer = (me + step) % count
        pltpu.make_async_remote_copy(
            src_ref=all_ref.at[me],
            dst_ref=all_ref.at[me],
            send_sem=send_sem,
            recv_sem=recv_sem,
            device_id=(peer // stripes, peer % stripes),
            device_id_type=MESH,
        ).start()
        return carry

    lax.fori_loop(1, count, send, 0)
    return size


def norm_terms(count, size, all_ref, send_sem, recv_sem, gain):
    others = all_ref.at[pl.ds(0, count - 1)]
    pltpu.make_async_copy(others, others, recv_sem).wait()
    pltpu.make_async_copy(others, others, send_sem).wait()
    stats = all_ref[...]
    chans = stats.shape[-1]
    half = chans // GROUPS // 2
    total = jnp.sum(stats, axis=0)
    gap = stats - total / count
    gaps = jnp.sum(gap * gap, axis=0)
    total = rows_of_8(total)
    gaps = rows_of_8(gaps)
    means = is_mean_lane(total.shape)
    mean = group_total(jnp.where(means, total, 0.0)) / (half * count)
    spread = group_total(jnp.where(means, gaps * size, total)) / half / (size * count)
    return mean[:1], (lax.rsqrt(spread + EPS) * gain)[:1]


def block_kernel(
    sections,
    stripes,
    feat_ref,
    gain1_ref,
    bias1_ref,
    weight_ref,
    bias_ref,
    gain2_ref,
    bias2_ref,
    wq_ref,
    wk_ref,
    wv_ref,
    resid_ref,
    attn_ref,
    ext,
    act,
    weight,
    conv,
    all1,
    all2,
    window,
    query,
    key,
    value,
    top,
    total,
    mixed,
    reply,
    stat_sem,
    weight_sem,
    out_sem,
    in_sem,
    window_out,
    window_in,
    back_out,
    back_in,
):
    count = sections * stripes
    tm = lax.axis_index("tm")
    row = lax.axis_index("rows")
    me = tm * stripes + row
    frames, high, width, chans = feat_ref.shape
    has_next = tm < sections - 1
    has_past = tm > 0
    has_above = row > 0
    has_below = row < stripes - 1

    loads = [
        pltpu.make_async_copy(weight_ref.at[a], weight.at[a], weight_sem.at[a]) for a in range(3)
    ]
    for load in loads:
        load.start()
    greet_all(count, stripes, me)

    def push(src, dst, slot, to_tm, to_row):
        return pltpu.make_async_remote_copy(
            src_ref=src,
            dst_ref=dst,
            send_sem=out_sem.at[slot],
            recv_sem=in_sem.at[slot],
            device_id=(to_tm, to_row),
            device_id_type=MESH,
        )

    now = pl.ds(frames, frames)
    past = pl.ds(0, frames)
    down = push(feat_ref.at[:, high - 1], ext.at[now, 0], 0, tm, row + 1)
    up = push(feat_ref.at[:, 0], ext.at[now, high + 1], 1, tm, row - 1)
    later = push(feat_ref, ext.at[past, pl.ds(1, high)], 2, tm + 1, row)
    later_top = push(ext.at[now, 0], ext.at[past, 0], 3, tm + 1, row)
    later_low = push(ext.at[now, high + 1], ext.at[past, high + 1], 4, tm + 1, row)

    pl.when(has_below)(lambda: down.start())
    pl.when(has_above)(lambda: up.start())
    pl.when(has_next)(lambda: later.start())

    blocks = [
        lambda f=f, o=o: feat_ref[f, o].astype(jnp.float32)
        for f in range(frames)
        for o in range(high)
    ]
    size = share_stats(count, stripes, me, blocks, all1, stat_sem.at[0], stat_sem.at[1])
    mean1, gain1 = norm_terms(count, size, all1, stat_sem.at[0], stat_sem.at[1], gain1_ref[...])
    bias1 = bias1_ref[...]
    column = lax.broadcasted_iota(jnp.int32, (width, chans), 0)

    def activate(source, targets):
        scaled = (source.astype(jnp.float32) - mean1) * gain1 + bias1
        half = 0.5 * scaled
        silu = half + half * jnp.tanh(half)
        before = jnp.where(column == 0, 0.0, pltpu.roll(silu, 1, 0)).astype(jnp.bfloat16)
        after = jnp.where(column == width - 1, 0.0, pltpu.roll(silu, width - 1, 0)).astype(
            jnp.bfloat16
        )
        here = silu.astype(jnp.bfloat16)
        for f, r in targets:
            act[f, r, :, :chans] = before
            act[f, r, :, chans : 2 * chans] = here
            act[f, r, :, 2 * chans :] = after

    def open_frames(r):
        for f in range(frames):
            act[f, r] = act[frames, r]

    for r in range(1, high + 1):
        for f in range(frames):
            activate(feat_ref[f, r - 1], [(frames + f, r)])
    pl.when(tm == 0)(lambda: [open_frames(r) for r in range(1, high + 1)] and None)

    @pl.when(has_past)
    def _():
        later.wait_recv()

        def earlier(index, carry):
            f = index // high
            r = 1 + index % high
            activate(ext[f, r], [(f, r)])
            return carry

        lax.fori_loop(0, frames * high, earlier, 0)

    cells = frames * width

    def taps(a, r, b):
        return jnp.dot(
            act[pl.ds(a, frames), r].reshape(cells, 3 * chans),
            weight[a, b],
            preferred_element_type=jnp.float32,
        ).reshape(frames, width, chans)

    conv[...] = jnp.broadcast_to(bias_ref[...].reshape(1, 1, 1, chans), conv.shape)

    def inner(a, carry):
        conv[:, 0] += taps(a, 1, 1) + taps(a, 2, 2)
        conv[:, 1] += taps(a, 1, 0) + taps(a, 2, 1)
        return carry

    for a in range(3):
        loads[a].wait()
    lax.fori_loop(0, 2, inner, 0)

    @pl.when(has_above)
    def _():
        down.wait_recv()
        pl.when(has_next)(lambda: later_top.start())

    @pl.when(has_below)
    def _():
        up.wait_recv()
        pl.when(has_next)(lambda: later_low.start())

    lax.fori_loop(2, 3, inner, 0)

    def halo(r, exists, relay):
        @pl.when(exists)
        def _():
            def each(f, carry):
                activate(ext[frames + f, r], [(frames + f, r)])
                return carry

            lax.fori_loop(0, frames, each, 0)
            pl.when(tm == 0)(lambda: open_frames(r))

            @pl.when(has_past)
            def _():
                relay.wait_recv()

                def each_past(f, carry):
                    activate(ext[f, r], [(f, r)])
                    return carry

                lax.fori_loop(0, frames, each_past, 0)

        @pl.when(jnp.logical_not(exists))
        def _():
            act[:, r] = jnp.zeros_like(act[:, r])

    halo(0, has_above, later_top)
    halo(high + 1, has_below, later_low)

    def outer(a, carry):
        conv[:, 0] += taps(a, 0, 0)
        conv[:, 1] += taps(a, high + 1, 2)
        return carry

    lax.fori_loop(0, 3, outer, 0)

    for f in range(frames):
        for o in range(high):
            resid_ref[f, pl.ds(o * width, width)] = (
                feat_ref[f, o].astype(jnp.float32) + conv[f, o]
            ).astype(jnp.bfloat16)

    k = row % BAND
    first = row - k
    half = k // 2
    has_band_above = first > 0
    has_band_below = first + BAND < stripes
    scale = 1.0 / math.sqrt(chans)

    def send(src, dst, sent, got, to_tm, to_row):
        return pltpu.make_async_remote_copy(
            src_ref=src,
            dst_ref=dst,
            send_sem=sent,
            recv_sem=got,
            device_id=(to_tm, to_row),
            device_id_type=MESH,
        )

    def scatter(j):
        return send(
            resid_ref.at[j],
            window.at[BAND + k],
            window_out.at[j],
            window_in.at[BAND + k],
            half,
            first + 2 * tm + j,
        )

    for j in range(2):
        pl.when(2 * tm + j != k)(lambda j=j: scatter(j).start())

        @pl.when(2 * tm + j == k)
        def _(j=j):
            pltpu.make_async_copy(
                resid_ref.at[j], window.at[BAND + k], window_in.at[BAND + k]
            ).start()

    blocks = [
        lambda f=f, o=o: resid_ref[f, pl.ds(o * width, width)].astype(jnp.float32)
        for f in range(frames)
        for o in range(high)
    ]
    size = share_stats(count, stripes, me, blocks, all2, stat_sem.at[2], stat_sem.at[3])

    pl.when(has_below)(lambda: down.wait_send())
    pl.when(has_above)(lambda: up.wait_send())

    @pl.when(has_next)
    def _():
        later.wait_send()
        pl.when(has_above)(lambda: later_top.wait_send())
        pl.when(has_below)(lambda: later_low.wait_send())

    mean2, gain2 = norm_terms(count, size, all2, stat_sem.at[2], stat_sem.at[3], gain2_ref[...])
    bias2 = bias2_ref[...]

    def arrived(slot):
        pltpu.make_async_copy(window.at[slot], window.at[slot], window_in.at[slot]).wait()

    def across(slot, number):
        return send(
            window.at[slot],
            window.at[slot],
            window_out.at[number],
            window_in.at[slot],
            1 - tm,
            row,
        )

    def downward(slot, number):
        return send(
            window.at[slot],
            window.at[slot - BAND],
            window_out.at[number],
            window_in.at[slot - BAND],
            tm,
            row + BAND,
        )

    def upward(slot, number):
        return send(
            window.at[slot],
            window.at[slot + BAND],
            window_out.at[number],
            window_in.at[slot + BAND],
            tm,
            row - BAND,
        )

    def normed(slot):
        return ((window[slot].astype(jnp.float32) - mean2) * gain2 + bias2).astype(jnp.bfloat16)

    def against(left, right):
        return lax.dot_general(
            left, right, (((1,), (1,)), ((), ())), preferred_element_type=jnp.float32
        )

    def queries(t, carry):
        i = (t + k) % 2
        slot = BAND + 2 * tm + i
        arrived(slot)
        pl.when(has_band_below)(lambda: downward(slot, 2 + i).start())
        pl.when(has_band_above)(lambda: upward(slot, 4 + i).start())
        across(slot, 6 + i).start()
        query[i] = jnp.dot(normed(slot), wq_ref[...], preferred_element_type=jnp.float32).astype(
            jnp.bfloat16
        )
        return carry

    lax.fori_loop(0, 2, queries, 0)
    top[...] = jnp.full_like(top, -1e30)
    total[...] = jnp.zeros_like(total)
    mixed[...] = jnp.zeros_like(mixed)

    def update(wanted):
        scores = [against(key[...], query[q]) for q in wanted]
        for q, score in zip(wanted, scores):
            old = top[q]
            new = jnp.maximum(old, jnp.max(score, axis=0, keepdims=True))
            expo = jnp.exp((score - new) * scale)
            shrink = jnp.exp((old - new) * scale)
            total[q] = total[q] * shrink + jnp.sum(expo, axis=0, keepdims=True)
            top[q] = new
            mixed[q] = mixed[q] * shrink + jnp.dot(
                value[...], expo.astype(jnp.bfloat16), preferred_element_type=jnp.float32
            )

    def slots(t, carry):
        paired = (t >= 4) & (t < 8)
        stage = jnp.where(paired, 2 + t % 2, jnp.where(t < 4, t // 2, 4))
        i = (jnp.where(paired, (t - 4) // 2, t % 2) + k) % 2
        slot = i + jnp.where(
            stage == 0,
            BAND + 2 * tm,
            jnp.where(
                stage == 1,
                BAND + 2 * (1 - tm),
                jnp.where(
                    stage == 2,
                    jnp.where(tm == 1, 2, 2 * BAND),
                    jnp.where(stage == 3, jnp.where(tm == 1, 2 * BAND + 2, 0), 2 + 6 * tm),
                ),
            ),
        )
        inside = ((slot >= BAND) | has_band_above) & ((slot < 2 * BAND) | has_band_below)

        @pl.when(inside)
        def _():
            pl.when(stage > 0)(lambda: arrived(slot))
            pl.when(stage == 2)(lambda: across(slot, 8 + i).start())
            cells_here = normed(slot)
            key[...] = jnp.dot(
                cells_here, wk_ref[...], preferred_element_type=jnp.float32
            ).astype(jnp.bfloat16)
            value[...] = against(wv_ref[...], cells_here).astype(jnp.bfloat16)
            offset = slot - 2 * tm
            pl.when((offset >= 1) & (offset <= 2 * BAND))(lambda: update((0, 1)))
            pl.when(offset == 0)(lambda: update((0,)))
            pl.when(offset == 2 * BAND + 1)(lambda: update((1,)))

        return carry

    lax.fori_loop(0, 10, slots, 0)

    def answer(q):
        return send(
            reply.at[q],
            attn_ref.at[k % 2],
            back_out.at[q],
            back_in.at[k % 2],
            half,
            first + 2 * tm + q,
        )

    for q in range(2):
        reply[q] = jnp.transpose(mixed[q] / total[q]).astype(jnp.bfloat16)
        pl.when(2 * tm + q != k)(lambda q=q: answer(q).start())

        @pl.when(2 * tm + q == k)
        def _(q=q):
            pltpu.make_async_copy(reply.at[q], attn_ref.at[k % 2], back_in.at[k % 2]).start()

    for j in range(2):
        pltpu.make_async_copy(attn_ref.at[j], attn_ref.at[j], back_in.at[j]).wait()

        @pl.when(2 * tm + j != k)
        def _(j=j):
            scatter(j).wait_send()
            answer(j).wait_send()

        across(BAND + 2 * tm + j, 6 + j).wait_send()
        pl.when(has_band_below)(lambda j=j: downward(BAND + 2 * tm + j, 2 + j).wait_send())
        pl.when(has_band_above)(lambda j=j: upward(BAND + 2 * tm + j, 4 + j).wait_send())
        pl.when((tm == 1) & has_band_above)(lambda j=j: across(2 + j, 8 + j).wait_send())
        pl.when((tm == 0) & has_band_below)(lambda j=j: across(2 * BAND + j, 8 + j).wait_send())


def shards(
    feat,
    norm1_gain,
    norm1_bias,
    conv_weight,
    conv_bias,
    norm2_gain,
    norm2_bias,
    w_query,
    w_key,
    w_value,
    w_out,
    out_bias,
):
    frames, high, width, chans = feat.shape
    sections = lax.axis_size("tm")
    stripes = lax.axis_size("rows")
    count = sections * stripes
    vmem = pl.BlockSpec(memory_space=pltpu.VMEM)
    anywhere = pl.BlockSpec(memory_space=pl.ANY)
    dma = pltpu.SemaphoreType.DMA
    cells = high * width
    image = jax.ShapeDtypeStruct((frames, cells, chans), jnp.bfloat16)
    resid, attn = pl.pallas_call(
        functools.partial(block_kernel, sections, stripes),
        out_shape=(image, image),
        in_specs=[vmem, vmem, vmem, anywhere] + [vmem] * 6,
        out_specs=(vmem, vmem),
        scratch_shapes=[
            pltpu.VMEM((2 * frames, high + 2, width, chans), jnp.bfloat16),
            pltpu.VMEM((2 * frames, high + 2, width, 3 * chans), jnp.bfloat16),
            pltpu.VMEM((3, 3, 3 * chans, chans), jnp.bfloat16),
            pltpu.VMEM((frames, high, width, chans), jnp.float32),
            pltpu.VMEM((count, 1, chans), jnp.float32),
            pltpu.VMEM((count, 1, chans), jnp.float32),
            pltpu.VMEM((3 * BAND, cells, chans), jnp.bfloat16),
            pltpu.VMEM((2, cells, chans), jnp.bfloat16),
            pltpu.VMEM((cells, chans), jnp.bfloat16),
            pltpu.VMEM((chans, cells), jnp.bfloat16),
            pltpu.VMEM((2, 1, cells), jnp.float32),
            pltpu.VMEM((2, 1, cells), jnp.float32),
            pltpu.VMEM((2, chans, cells), jnp.float32),
            pltpu.VMEM((2, cells, chans), jnp.bfloat16),
            dma((4,)),
            dma((3,)),
            dma((5,)),
            dma((5,)),
            dma((10,)),
            dma((3 * BAND,)),
            dma((2,)),
            dma((2,)),
        ],
        compiler_params=pltpu.CompilerParams(
            collective_id=0, has_side_effects=True, vmem_limit_bytes=VMEM_LIMIT
        ),
        name="block",
    )(
        feat,
        norm1_gain[None],
        norm1_bias[None],
        conv_weight.reshape(3, 3, 3 * chans, chans),
        conv_bias[None],
        norm2_gain[None],
        norm2_bias[None],
        w_query,
        w_key,
        w_value.T,
    )
    output = jnp.dot(
        attn.reshape(-1, chans), w_out, preferred_element_type=jnp.float32
    ).reshape(frames, high, width, chans)
    resid = resid.reshape(feat.shape).astype(jnp.float32)
    return (resid + out_bias + output).astype(jnp.bfloat16)


def solution(mesh):
    return jax.shard_map(
        shards,
        mesh=mesh,
        in_specs=(
            P("tm", "rows", None, None),
            P(),
            P(),
            P(),
            P(),
            P(),
            P(),
            P(),
            P(),
            P(),
            P(),
            P(),
        ),
        out_specs=P("tm", "rows", None, None),
        check_vma=False,
    )
```

```python
import functools
import math

import jax
import jax.numpy as jnp
from jax import lax
from jax.experimental import pallas as pl
from jax.experimental.pallas import tpu as pltpu
from jax.sharding import PartitionSpec as P

GROUPS = 32
EPS = 1e-06
BAND = 4
MESH = pl.DeviceIdType.MESH
VMEM_LIMIT = 56 * 1024 * 1024


def greet_all(count, stripes, me):
    barrier = pltpu.get_barrier_semaphore()

    def greet(step, carry):
        peer = (me + step) % count
        pl.semaphore_signal(
            barrier, inc=1, device_id=(peer // stripes, peer % stripes), device_id_type=MESH
        )
        return carry

    lax.fori_loop(1, count, greet, 0)
    pl.semaphore_wait(barrier, count - 1)


def group_total(values):
    chans = values.shape[-1]
    each = chans // GROUPS
    lane = lax.broadcasted_iota(jnp.int32, values.shape, 1)
    step = 1
    while step < each:
        ahead = pltpu.roll(values, chans - step, 1)
        behind = pltpu.roll(values, step, 1)
        values = values + jnp.where((lane // step) % 2 == 0, ahead, behind)
        step *= 2
    return values


def rows_of_8(line):
    return jnp.broadcast_to(line, (8, line.shape[-1]))


def is_mean_lane(shape):
    each = shape[-1] // GROUPS
    return lax.broadcasted_iota(jnp.int32, shape, 1) % each < each // 2


def share_stats(count, stripes, me, blocks, all_ref, send_sem, recv_sem):
    first = blocks[0]()
    chans = first.shape[-1]
    size = len(blocks) * first.shape[0] * (chans // GROUPS)
    total = jnp.sum(first, axis=0, keepdims=True)
    for block in blocks[1:]:
        total = total + jnp.sum(block(), axis=0, keepdims=True)
    mean = group_total(rows_of_8(total)) / size
    spread = jnp.zeros((1, chans), jnp.float32)
    for block in blocks:
        gap = block() - mean[:1]
        spread = spread + jnp.sum(gap * gap, axis=0, keepdims=True)
    spread = group_total(rows_of_8(spread))
    all_ref[me] = jnp.where(is_mean_lane(mean.shape), mean, spread)[:1]

    def send(step, carry):
        peer = (me + step) % count
        pltpu.make_async_remote_copy(
            src_ref=all_ref.at[me],
            dst_ref=all_ref.at[me],
            send_sem=send_sem,
            recv_sem=recv_sem,
            device_id=(peer // stripes, peer % stripes),
            device_id_type=MESH,
        ).start()
        return carry

    lax.fori_loop(1, count, send, 0)
    return size


def norm_terms(count, size, all_ref, send_sem, recv_sem, gain):
    others = all_ref.at[pl.ds(0, count - 1)]
    pltpu.make_async_copy(others, others, recv_sem).wait()
    pltpu.make_async_copy(others, others, send_sem).wait()
    stats = all_ref[...]
    chans = stats.shape[-1]
    half = chans // GROUPS // 2
    total = jnp.sum(stats, axis=0)
    gap = stats - total / count
    gaps = jnp.sum(gap * gap, axis=0)
    total = rows_of_8(total)
    gaps = rows_of_8(gaps)
    means = is_mean_lane(total.shape)
    mean = group_total(jnp.where(means, total, 0.0)) / (half * count)
    spread = group_total(jnp.where(means, gaps * size, total)) / half / (size * count)
    return mean[:1], (lax.rsqrt(spread + EPS) * gain)[:1]


def block_kernel(
    sections,
    stripes,
    feat_ref,
    gain1_ref,
    bias1_ref,
    weight_ref,
    bias_ref,
    gain2_ref,
    bias2_ref,
    wq_ref,
    wk_ref,
    wv_ref,
    resid_ref,
    attn_ref,
    ext,
    act,
    weight,
    conv,
    all1,
    all2,
    window,
    query,
    key,
    value,
    top,
    total,
    mixed,
    reply,
    value_weight,
    stat_sem,
    weight_sem,
    out_sem,
    in_sem,
    window_out,
    window_in,
    back_out,
    back_in,
):
    count = sections * stripes
    tm = lax.axis_index("tm")
    row = lax.axis_index("rows")
    me = tm * stripes + row
    frames, high, width, chans = feat_ref.shape
    has_next = tm < sections - 1
    has_past = tm > 0
    has_above = row > 0
    has_below = row < stripes - 1

    loads = [
        pltpu.make_async_copy(weight_ref.at[a], weight.at[a], weight_sem.at[a]) for a in range(3)
    ]
    for load in loads:
        load.start()
    greet_all(count, stripes, me)

    def push(src, dst, slot, to_tm, to_row):
        return pltpu.make_async_remote_copy(
            src_ref=src,
            dst_ref=dst,
            send_sem=out_sem.at[slot],
            recv_sem=in_sem.at[slot],
            device_id=(to_tm, to_row),
            device_id_type=MESH,
        )

    past = pl.ds(0, frames)
    low = high + 1
    later = push(feat_ref, ext.at[past, pl.ds(1, high)], 0, tm + 1, row)
    down = []
    up = []
    top_on = []
    low_on = []
    for f in range(frames):
        n = 1 + 4 * f
        own = frames + f
        down.append(push(feat_ref.at[f, high - 1], ext.at[own, 0], n, tm, row + 1))
        up.append(push(feat_ref.at[f, 0], ext.at[own, low], n + 1, tm, row - 1))
        top_on.append(push(ext.at[own, 0], ext.at[f, 0], n + 2, tm + 1, row))
        low_on.append(push(ext.at[own, low], ext.at[f, low], n + 3, tm + 1, row))

    def send_edges(f):
        pl.when(has_below)(lambda: down[f].start())
        pl.when(has_above)(lambda: up[f].start())

    send_edges(0)
    pl.when(has_next)(lambda: later.start())

    blocks = [
        lambda f=f, o=o: feat_ref[f, o].astype(jnp.float32)
        for f in range(frames)
        for o in range(high)
    ]
    size = share_stats(count, stripes, me, blocks, all1, stat_sem.at[0], stat_sem.at[1])
    for f in range(1, frames):
        send_edges(f)
    value_weight[...] = jnp.transpose(wv_ref[...])
    mean1, gain1 = norm_terms(count, size, all1, stat_sem.at[0], stat_sem.at[1], gain1_ref[...])
    bias1 = bias1_ref[...]
    column = lax.broadcasted_iota(jnp.int32, (width, chans), 0)

    def activate(source, targets):
        scaled = (source.astype(jnp.float32) - mean1) * gain1 + bias1
        half = 0.5 * scaled
        silu = half + half * jnp.tanh(half)
        before = jnp.where(column == 0, 0.0, pltpu.roll(silu, 1, 0)).astype(jnp.bfloat16)
        after = jnp.where(column == width - 1, 0.0, pltpu.roll(silu, width - 1, 0)).astype(
            jnp.bfloat16
        )
        here = silu.astype(jnp.bfloat16)
        for f, r in targets:
            act[f, r, :, :chans] = before
            act[f, r, :, chans : 2 * chans] = here
            act[f, r, :, 2 * chans :] = after

    def open_frames(r):
        for f in range(frames):
            act[f, r] = act[frames, r]

    for r in range(1, high + 1):
        for f in range(frames):
            activate(feat_ref[f, r - 1], [(frames + f, r)])
    pl.when(tm == 0)(lambda: [open_frames(r) for r in range(1, high + 1)] and None)

    @pl.when(has_past)
    def _():
        later.wait_recv()

        def earlier(index, carry):
            f = index // high
            r = 1 + index % high
            activate(ext[f, r], [(f, r)])
            return carry

        lax.fori_loop(0, frames * high, earlier, 0)

    cells = frames * width

    def taps(a, r, b):
        return jnp.dot(
            act[pl.ds(a, frames), r].reshape(cells, 3 * chans),
            weight[a, b],
            preferred_element_type=jnp.float32,
        ).reshape(frames, width, chans)

    conv[...] = jnp.broadcast_to(bias_ref[...].reshape(1, 1, 1, chans), conv.shape)

    def inner(a, carry):
        conv[:, 0] += taps(a, 1, 1) + taps(a, 2, 2)
        conv[:, 1] += taps(a, 1, 0) + taps(a, 2, 1)
        return carry

    for a in range(3):
        loads[a].wait()
    def pass_on(f):
        @pl.when(has_next & has_above)
        def _():
            down[f].wait_recv()
            top_on[f].start()

        @pl.when(has_next & has_below)
        def _():
            up[f].wait_recv()
            low_on[f].start()

    lax.fori_loop(0, 2, inner, 0)
    pass_on(0)
    lax.fori_loop(2, 3, inner, 0)
    pass_on(1)

    def tap(e, r, f):
        o, b = (0, 0) if r == 0 else (high - 1, 2)
        conv[f, o] += jnp.dot(act[e, r], weight[e - f, b], preferred_element_type=jnp.float32)

    edges = ((0, has_above, down, top_on), (low, has_below, up, low_on))

    def first_edges(r, exists, near, relay):
        @pl.when(exists)
        def _():
            pl.when(has_past)(lambda: near[0].wait_recv())
            activate(ext[2, r], [(2, r)])
            tap(2, r, 0)
            tap(2, r, 1)

            @pl.when(tm == 0)
            def _():
                act[0, r] = act[2, r]
                act[1, r] = act[2, r]
                tap(1, r, 0)
                tap(1, r, 1)

            @pl.when(has_past)
            def _():
                relay[0].wait_recv()
                activate(ext[0, r], [(0, r)])

            tap(0, r, 0)

    def last_edges(r, exists, near, relay):
        @pl.when(exists)
        def _():
            pl.when(has_past)(lambda: near[1].wait_recv())
            activate(ext[3, r], [(3, r)])
            tap(3, r, 1)

            @pl.when(has_past)
            def _():
                relay[1].wait_recv()
                activate(ext[1, r], [(1, r)])
                tap(1, r, 0)
                tap(1, r, 1)

    def settle(f):
        for o in range(high):
            resid_ref[f, pl.ds(o * width, width)] = (
                feat_ref[f, o].astype(jnp.float32) + conv[f, o]
            ).astype(jnp.bfloat16)

    k = row % BAND
    first = row - k
    half = k // 2
    has_band_above = first > 0
    has_band_below = first + BAND < stripes
    scale = 1.0 / math.sqrt(chans)

    def send(src, dst, sent, got, to_tm, to_row):
        return pltpu.make_async_remote_copy(
            src_ref=src,
            dst_ref=dst,
            send_sem=sent,
            recv_sem=got,
            device_id=(to_tm, to_row),
            device_id_type=MESH,
        )

    def scatter(j):
        return send(
            resid_ref.at[j],
            window.at[BAND + k],
            window_out.at[j],
            window_in.at[BAND + k],
            half,
            first + 2 * tm + j,
        )

    def leave(j):
        settle(j)
        pl.when(2 * tm + j != k)(lambda: scatter(j).start())

        @pl.when(2 * tm + j == k)
        def _():
            pltpu.make_async_copy(
                resid_ref.at[j], window.at[BAND + k], window_in.at[BAND + k]
            ).start()

    for edge in edges:
        first_edges(*edge)
    pl.when(tm == 0)(lambda: leave(0))
    for edge in edges:
        last_edges(*edge)
    pl.when(has_past)(lambda: leave(0))
    leave(1)

    blocks = [
        lambda f=f, o=o: resid_ref[f, pl.ds(o * width, width)].astype(jnp.float32)
        for f in range(frames)
        for o in range(high)
    ]
    size = share_stats(count, stripes, me, blocks, all2, stat_sem.at[2], stat_sem.at[3])

    for f in range(frames):
        pl.when(has_below)(lambda f=f: down[f].wait_send())
        pl.when(has_above)(lambda f=f: up[f].wait_send())
        pl.when(has_next & has_above)(lambda f=f: top_on[f].wait_send())
        pl.when(has_next & has_below)(lambda f=f: low_on[f].wait_send())
    pl.when(has_next)(lambda: later.wait_send())

    mean2, gain2 = norm_terms(count, size, all2, stat_sem.at[2], stat_sem.at[3], gain2_ref[...])
    bias2 = bias2_ref[...]

    def arrived(slot):
        pltpu.make_async_copy(window.at[slot], window.at[slot], window_in.at[slot]).wait()

    def across(slot, number):
        return send(
            window.at[slot],
            window.at[slot],
            window_out.at[number],
            window_in.at[slot],
            1 - tm,
            row,
        )

    def downward(slot, number):
        return send(
            window.at[slot],
            window.at[slot - BAND],
            window_out.at[number],
            window_in.at[slot - BAND],
            tm,
            row + BAND,
        )

    def upward(slot, number):
        return send(
            window.at[slot],
            window.at[slot + BAND],
            window_out.at[number],
            window_in.at[slot + BAND],
            tm,
            row - BAND,
        )

    def normed(slot):
        return ((window[slot].astype(jnp.float32) - mean2) * gain2 + bias2).astype(jnp.bfloat16)

    def against(left, right):
        return lax.dot_general(
            left, right, (((1,), (1,)), ((), ())), preferred_element_type=jnp.float32
        )

    def queries(t, carry):
        i = (t + k) % 2
        slot = BAND + 2 * tm + i
        arrived(slot)
        pl.when(has_band_below)(lambda: downward(slot, 2 + i).start())
        pl.when(has_band_above)(lambda: upward(slot, 4 + i).start())
        across(slot, 6 + i).start()
        query[i] = jnp.dot(normed(slot), wq_ref[...], preferred_element_type=jnp.float32).astype(
            jnp.bfloat16
        )
        return carry

    lax.fori_loop(0, 2, queries, 0)
    top[...] = jnp.full_like(top, -1e30)
    total[...] = jnp.zeros_like(total)
    mixed[...] = jnp.zeros_like(mixed)

    def update(wanted):
        scores = [against(key[...], query[q]) for q in wanted]
        for q, score in zip(wanted, scores):
            old = top[q]
            new = jnp.maximum(old, jnp.max(score, axis=0, keepdims=True))
            expo = jnp.exp((score - new) * scale)
            shrink = jnp.exp((old - new) * scale)
            total[q] = total[q] * shrink + jnp.sum(expo, axis=0, keepdims=True)
            top[q] = new
            mixed[q] = mixed[q] * shrink + jnp.dot(
                value[...], expo.astype(jnp.bfloat16), preferred_element_type=jnp.float32
            )

    def slots(t, carry):
        paired = (t >= 4) & (t < 8)
        stage = jnp.where(paired, 2 + t % 2, jnp.where(t < 4, t // 2, 4))
        i = (jnp.where(paired, (t - 4) // 2, t % 2) + k) % 2
        slot = i + jnp.where(
            stage == 0,
            BAND + 2 * tm,
            jnp.where(
                stage == 1,
                BAND + 2 * (1 - tm),
                jnp.where(
                    stage == 2,
                    jnp.where(tm == 1, 2, 2 * BAND),
                    jnp.where(stage == 3, jnp.where(tm == 1, 2 * BAND + 2, 0), 2 + 6 * tm),
                ),
            ),
        )
        inside = ((slot >= BAND) | has_band_above) & ((slot < 2 * BAND) | has_band_below)

        @pl.when(inside)
        def _():
            pl.when(stage > 0)(lambda: arrived(slot))
            pl.when(stage == 2)(lambda: across(slot, 8 + i).start())
            cells_here = normed(slot)
            key[...] = jnp.dot(
                cells_here, wk_ref[...], preferred_element_type=jnp.float32
            ).astype(jnp.bfloat16)
            value[...] = against(value_weight[...], cells_here).astype(jnp.bfloat16)
            offset = slot - 2 * tm
            pl.when((offset >= 1) & (offset <= 2 * BAND))(lambda: update((0, 1)))
            pl.when(offset == 0)(lambda: update((0,)))
            pl.when(offset == 2 * BAND + 1)(lambda: update((1,)))

        return carry

    lax.fori_loop(0, 10, slots, 0)

    def answer(q):
        return send(
            reply.at[q],
            attn_ref.at[k % 2],
            back_out.at[q],
            back_in.at[k % 2],
            half,
            first + 2 * tm + q,
        )

    for q in range(2):
        reply[q] = jnp.transpose(mixed[q] / total[q]).astype(jnp.bfloat16)
        pl.when(2 * tm + q != k)(lambda q=q: answer(q).start())

        @pl.when(2 * tm + q == k)
        def _(q=q):
            pltpu.make_async_copy(reply.at[q], attn_ref.at[k % 2], back_in.at[k % 2]).start()

    for j in range(2):
        pltpu.make_async_copy(attn_ref.at[j], attn_ref.at[j], back_in.at[j]).wait()

        @pl.when(2 * tm + j != k)
        def _(j=j):
            scatter(j).wait_send()
            answer(j).wait_send()

        across(BAND + 2 * tm + j, 6 + j).wait_send()
        pl.when(has_band_below)(lambda j=j: downward(BAND + 2 * tm + j, 2 + j).wait_send())
        pl.when(has_band_above)(lambda j=j: upward(BAND + 2 * tm + j, 4 + j).wait_send())
        pl.when((tm == 1) & has_band_above)(lambda j=j: across(2 + j, 8 + j).wait_send())
        pl.when((tm == 0) & has_band_below)(lambda j=j: across(2 * BAND + j, 8 + j).wait_send())


def shards(
    feat,
    norm1_gain,
    norm1_bias,
    conv_weight,
    conv_bias,
    norm2_gain,
    norm2_bias,
    w_query,
    w_key,
    w_value,
    w_out,
    out_bias,
):
    frames, high, width, chans = feat.shape
    sections = lax.axis_size("tm")
    stripes = lax.axis_size("rows")
    count = sections * stripes
    vmem = pl.BlockSpec(memory_space=pltpu.VMEM)
    anywhere = pl.BlockSpec(memory_space=pl.ANY)
    dma = pltpu.SemaphoreType.DMA
    cells = high * width
    image = jax.ShapeDtypeStruct((frames, cells, chans), jnp.bfloat16)
    resid, attn = pl.pallas_call(
        functools.partial(block_kernel, sections, stripes),
        out_shape=(image, image),
        in_specs=[vmem, vmem, vmem, anywhere] + [vmem] * 6,
        out_specs=(vmem, vmem),
        scratch_shapes=[
            pltpu.VMEM((2 * frames, high + 2, width, chans), jnp.bfloat16),
            pltpu.VMEM((2 * frames, high + 2, width, 3 * chans), jnp.bfloat16),
            pltpu.VMEM((3, 3, 3 * chans, chans), jnp.bfloat16),
            pltpu.VMEM((frames, high, width, chans), jnp.float32),
            pltpu.VMEM((count, 1, chans), jnp.float32),
            pltpu.VMEM((count, 1, chans), jnp.float32),
            pltpu.VMEM((3 * BAND, cells, chans), jnp.bfloat16),
            pltpu.VMEM((2, cells, chans), jnp.bfloat16),
            pltpu.VMEM((cells, chans), jnp.bfloat16),
            pltpu.VMEM((chans, cells), jnp.bfloat16),
            pltpu.VMEM((2, 1, cells), jnp.float32),
            pltpu.VMEM((2, 1, cells), jnp.float32),
            pltpu.VMEM((2, chans, cells), jnp.float32),
            pltpu.VMEM((2, cells, chans), jnp.bfloat16),
            pltpu.VMEM((chans, chans), jnp.bfloat16),
            dma((4,)),
            dma((3,)),
            dma((9,)),
            dma((9,)),
            dma((10,)),
            dma((3 * BAND,)),
            dma((2,)),
            dma((2,)),
        ],
        compiler_params=pltpu.CompilerParams(
            collective_id=0, has_side_effects=True, vmem_limit_bytes=VMEM_LIMIT
        ),
        name="block",
    )(
        feat,
        norm1_gain[None],
        norm1_bias[None],
        conv_weight.reshape(3, 3, 3 * chans, chans),
        conv_bias[None],
        norm2_gain[None],
        norm2_bias[None],
        w_query,
        w_key,
        w_value,
    )
    output = jnp.dot(
        attn.reshape(-1, chans), w_out, preferred_element_type=jnp.float32
    ).reshape(frames, high, width, chans)
    resid = resid.reshape(feat.shape).astype(jnp.float32)
    return (resid + out_bias + output).astype(jnp.bfloat16)


def solution(mesh):
    return jax.shard_map(
        shards,
        mesh=mesh,
        in_specs=(
            P("tm", "rows", None, None),
            P(),
            P(),
            P(),
            P(),
            P(),
            P(),
            P(),
            P(),
            P(),
            P(),
            P(),
        ),
        out_specs=P("tm", "rows", None, None),
        check_vma=False,
    )
```
